32 devices in a mesh: grp: 2 (over y), ex: 8 (over z, core), lay: 2 (over x).
Axes of the slice: x: 2, y: 2, z: 4, core: 2. Of those that a mesh axis runs over, the one named last changes fastest.
Arguments:
- train_grads: bfloat16 [2, 8192, 4096], P('lay', ('grp', 'ex')), parts along dimension 1, may hold values from -0.0625 to 0.0625
- query_grads: bfloat16 [2, 512, 4096], P('lay', ('grp', 'ex')), parts along dimension 1, may hold values from -6 to 6
- out_basis: float32 [2, 64, 64], P('lay'), may hold values from -0.75 to 0.75
- in_basis: float32 [2, 64, 64], P('lay'), may hold values from -0.75 to 0.75
- eigenvalues: float32 [2, 64, 64], P('lay'), may hold values from 0.05 to 5
Outputs:
- scores: float32 [8192, 256], P(('grp', 'ex'), 'lay'), parts along dimension 0
The draws below stay inside these ranges and needn't reach their ends.
There are 2 independent parts, one for each index of `grp`. The reference program is written for one: setup_inputs(seed, part) draws one part's arguments, and reference() takes and returns one part's arrays. A program takes and returns all parts, laid end to end along the dimension named above; an argument that names none is the same for every part. Nothing has to cross between parts.
All inputs are finite; a program needn't handle non-finite values.
Results may differ from the reference program's by a relative error of at most 0.0029.
Values may be sent and summed in bfloat16 or wider, within the bound.
A program may use at most 64 MiB of HBM per device.

```python
import math
import jax
import jax.numpy as jnp
from jax import lax

KO = 64
KI = 64
P_SIZE = 4096
EXAMPLES = 4096
QUERIES = 256
LAYERS = 2


def spiked(entries, stream_key, source, target, parts, factor):
    owner, partner = [(jnp.arange(entries.shape[dim]) // (entries.shape[dim] // parts)).reshape([-1 if axis == dim else 1 for axis in range(entries.ndim)]) for dim in (source, target)]
    chosen = jax.random.permutation(stream_key, parts)[partner]
    strong = (owner == chosen) | (owner == (partner + parts // 2) % parts)
    return jnp.where(strong, factor * entries, entries)


def block_levels(key, dims, pieces, smallest, high):
    def one(dim, blocks):
        heights = jax.random.uniform(jax.random.fold_in(jax.random.fold_in(key, 6), dim), (blocks,), jnp.float32, smallest / len(pieces), high / len(pieces))
        return jnp.repeat(jnp.exp(heights), dims[dim] // blocks).reshape((-1,) + (1,) * (len(dims) - dim - 1))

    factor_of = one(*pieces[0])
    for cut in pieces[1:]:
        factor_of = factor_of * one(*cut)
    return factor_of


def normal_values(stream_key, shape, deviation, bound, shards=(), kind=jnp.bfloat16):
    level = block_levels(stream_key, shape, shards, -0.22, 0.18) if shards else 1.0
    array = jax.random.normal(stream_key, shape, jnp.float32) * deviation * level
    return jnp.minimum(jnp.maximum(array, -bound), bound).astype(kind)


def noise_with(key, dims, deviation, reach, pieces, heavy, kind=jnp.bfloat16):
    array = deviation * jax.random.normal(key, dims, jnp.float32)
    if pieces:
        array = array * block_levels(key, dims, pieces, -0.22, 0.18)
    return jnp.clip(spiked(array, jax.random.fold_in(key, 3), *heavy), -reach, reach).astype(kind)


def setup_inputs(seed: int = 0, part: int = 0) -> dict:
    keys = jax.random.split(jax.random.key(seed), 6)
    part_splits = jax.random.split(jax.random.fold_in(keys[5], part), 6)
    return {
        "train_grads": normal_values(part_splits[0], (LAYERS, EXAMPLES, P_SIZE), (P_SIZE * LAYERS) ** -0.5, 0.0625, ((0, 2), (1, 8))),
        "query_grads": noise_with(part_splits[1], (LAYERS, QUERIES, P_SIZE), 1.0, 6.0, ((0, 2), (1, 8)), (0, 1, 2, 2.0)),
        "out_basis": normal_values(keys[2], (LAYERS, KO, KO), KO ** -0.5, 0.75, ((0, 2),), jnp.float32),
        "in_basis": normal_values(keys[3], (LAYERS, KI, KI), KI ** -0.5, 0.75, ((0, 2),), jnp.float32),
        "eigenvalues": jnp.clip(jnp.exp(math.log(5.0) - 4.6051702 * jax.random.uniform(keys[4], (LAYERS, KO, KI), jnp.float32) ** block_levels(keys[4], (LAYERS, KO, KI), ((0, 2),), -0.2, 0.2)), 0.05, 5.0),
    }


DAMPING = 0.1


def precondition(queries, out_mat, in_mat, eig_table):
    grid = queries.astype(jnp.float32).reshape(queries.shape[0], KO, KI)
    inner = jnp.einsum("qac,cd->qad", grid, in_mat, precision=lax.Precision.HIGHEST)
    rotated = jnp.einsum("ab,qad->qbd", out_mat, inner, precision=lax.Precision.HIGHEST)
    rotated = rotated / (eig_table + DAMPING)
    back = jnp.einsum("qbd,cd->qbc", rotated, in_mat, precision=lax.Precision.HIGHEST)
    result = jnp.einsum("ab,qbc->qac", out_mat, back, precision=lax.Precision.HIGHEST)
    return result.reshape(queries.shape[0], KO * KI).astype(jnp.bfloat16)


def reference(train_grads, query_grads, out_basis, in_basis, eigenvalues):
    total = jnp.zeros((EXAMPLES, QUERIES), jnp.float32)
    for layer in range(LAYERS):
        precond = precondition(query_grads[layer], out_basis[layer], in_basis[layer], eigenvalues[layer])
        total = total + lax.dot_general(train_grads[layer], precond, (((1,), (1,)), ((), ())), preferred_element_type=jnp.float32)
    return total
```

```python
import functools

import jax
import jax.numpy as jnp
from jax import lax
from jax.experimental import pallas as pl
from jax.experimental.pallas import tpu as pltpu
from jax.sharding import PartitionSpec as P

DAMPING = 0.1
CORES = 2
CHUNKS = 4
LANES = 128
F32, BF16 = jnp.float32, jnp.bfloat16
NN = (((1,), (0,)), ((), ()))
NT = (((1,), (1,)), ((), ()))


def dot(a, b, dims=NN):
    return lax.dot_general(a, b, dims, preferred_element_type=F32)


def split(x):
    high = x.astype(BF16)
    return high, (x - high.astype(F32)).astype(BF16)


def kernel(z_size, lay_size, train_hbm, query_ref, out_ref, in_ref, eig_ref, score_ref,
           train, held, by_tile, by_query, acc, own, stage, landed,
           train_sem, recv_line, recv_pair, send_line, send_pair, send_lay, recv_lay):
    ex, lay = lax.axis_index("ex"), lax.axis_index("lay")
    z, core = ex // CORES, ex % CORES
    count, width = query_ref.shape[1:]
    side = out_ref.shape[1]
    tiles = width // LANES
    columns = width // CHUNKS
    per_chunk = tiles // CHUNKS
    groups = z_size // lay_size
    has_left, has_right = z > 0, z < z_size - 1

    load = pltpu.make_async_copy(train_hbm.at[0], train, train_sem)
    load.start()

    barrier = pltpu.get_barrier_semaphore()

    def greet(target):
        pl.semaphore_signal(barrier, inc=1, device_id=target, device_id_type=pl.DeviceIdType.MESH)

    pl.when(has_left)(lambda: greet({"ex": ex - CORES}))
    pl.when(has_right)(lambda: greet({"ex": ex + CORES}))
    greet({"ex": z * CORES + 1 - core})
    for step in range(1, lay_size):
        greet({"lay": (lay + step) % lay_size})

    def line_copy(source, chunk, direction):
        block = held.at[source, chunk, pl.ds(pl.multiple_of(core * count, count), count)]
        return pltpu.make_async_remote_copy(
            block, block, send_line.at[source, chunk, (direction + 1) // 2], recv_line.at[source, chunk],
            device_id={"ex": ex + direction * CORES}, device_id_type=pl.DeviceIdType.MESH)

    def pair_copy(source, chunk, who):
        block = held.at[source, chunk, pl.ds(pl.multiple_of(who * count, count), count)]
        return pltpu.make_async_remote_copy(
            block, block, send_pair.at[source, chunk], recv_pair.at[source, chunk],
            device_id={"ex": z * CORES + 1 - core}, device_id_type=pl.DeviceIdType.MESH)

    def lay_copy(source):
        return pltpu.make_async_remote_copy(
            stage.at[source], landed.at[lay, source % groups], send_lay.at[source],
            recv_lay.at[lay, source % groups],
            device_id={"lay": source // groups}, device_id_type=pl.DeviceIdType.MESH)

    half = jnp.concatenate([in_ref[0], in_ref[0]], axis=1)
    low_lane = lax.broadcasted_iota(jnp.int32, half.shape, 1) < side
    zero = jnp.zeros_like(half)
    first, second = jnp.where(low_lane, half, 0.0), jnp.where(low_lane, 0.0, half)
    mix = jnp.concatenate([
        jnp.concatenate([first, zero], axis=1), jnp.concatenate([zero, first], axis=1),
        jnp.concatenate([second, zero], axis=1), jnp.concatenate([zero, second], axis=1)], axis=0)
    mix_high, mix_low = split(mix)
    rows = lax.broadcasted_iota(jnp.int32, (side, side), 0)
    cols = lax.broadcasted_iota(jnp.int32, (side, side), 1)
    order = (cols == 2 * (rows % tiles) + rows // tiles).astype(BF16)
    basis_high, basis_low = split(out_ref[0])
    sorted_high, sorted_low = dot(order, basis_high), dot(order, basis_low)
    to_eigen = jnp.concatenate([sorted_high.T, sorted_high.T, sorted_low.T], axis=1).astype(BF16)
    from_eigen = jnp.concatenate([sorted_high, sorted_high, sorted_low], axis=1).astype(BF16)
    scale = 1.0 / (eig_ref[0] + DAMPING)
    scale = jnp.concatenate([scale] * 4, axis=1)

    for p in range(tiles):
        by_tile[p * count:(p + 1) * count, :] = query_ref[0, :, p * LANES:(p + 1) * LANES].astype(F32)

    def stacked(x):
        high, low = split(x)
        return jnp.concatenate([high, low, high], axis=0)

    for quad in range(count // 4):
        pairs = jnp.concatenate([
            jnp.concatenate([by_tile[pl.ds(4 * quad + 2 * j + i, tiles, stride=count), :] for i in range(2)], axis=1)
            for j in range(2)], axis=0).astype(BF16)
        inner = dot(pairs, mix_high) + dot(pairs, mix_low)
        inner = jnp.concatenate([
            jnp.concatenate([inner[j * tiles:(j + 1) * tiles, s * LANES:(s + 1) * LANES] for j in range(2)], axis=1)
            for s in range(2)], axis=0)
        rotated = dot(to_eigen, stacked(inner)) * scale
        back = dot(from_eigen, stacked(rotated))
        back = jnp.concatenate([
            jnp.concatenate([back[s * tiles:(s + 1) * tiles, j * LANES:(j + 1) * LANES] for s in range(2)], axis=1)
            for j in range(2)], axis=0)
        high, low = split(back)
        result = dot(high, mix_high, NT) + dot(high, mix_low, NT) + dot(low, mix_high, NT)
        for j in range(2):
            for i in range(2):
                at = (4 * quad + 2 * j + i) * tiles
                by_query[at:at + tiles, :] = result[j * tiles:(j + 1) * tiles, i * LANES:(i + 1) * LANES]

    neighbours = has_left.astype(jnp.int32) + has_right.astype(jnp.int32) + lay_size
    pl.semaphore_wait(barrier, neighbours)

    mine = pl.ds(pl.multiple_of(core * count, count), count)
    for chunk in range(CHUNKS):
        for t in range(per_chunk):
            tile = by_query[pl.ds(chunk * per_chunk + t, count, stride=tiles), :]
            held[z, chunk, mine, t * LANES:(t + 1) * LANES] = tile.astype(BF16)
        pl.when(has_left)(lambda: line_copy(z, chunk, -1).start())
        pl.when(has_right)(lambda: line_copy(z, chunk, 1).start())
        pair_copy(z, chunk, core).start()

    def forward(source, chunk, direction, more):
        line_copy(source, chunk, direction).wait_recv()
        pl.when(more)(lambda: line_copy(source, chunk, direction).start())
        pair_copy(source, chunk, core).start()

    def multiply(source, chunk, slot):
        pair_copy(source, chunk, 1 - core).wait_recv()
        part = dot(held[source, chunk], train[:, chunk * columns:(chunk + 1) * columns], NT)
        if chunk > 0:
            part = part + acc[slot]
        if chunk < CHUNKS - 1:
            acc[slot] = part
        else:
            @pl.when(source // groups == lay)
            def _():
                own[source % groups] = part

            @pl.when(source // groups != lay)
            def _():
                stage[source] = part.astype(BF16)
                lay_copy(source).start()

    def multiply_both(distance, chunk):
        pl.when((distance >= 0) & (z + distance < z_size))(lambda: multiply(z + distance, chunk, 0))
        pl.when((distance >= 1) & (z - distance >= 0))(lambda: multiply(z - distance, chunk, 1))

    load.wait()

    def step(distance, carry):
        for chunk in range(CHUNKS):
            @pl.when((distance >= 1) & (z + distance < z_size))
            def _():
                forward(z + distance, chunk, -1, has_left)

            @pl.when((distance >= 1) & (z - distance >= 0))
            def _():
                forward(z - distance, chunk, 1, has_right)

            if chunk == 0:
                multiply_both(distance - 1, CHUNKS - 1)
            else:
                multiply_both(distance, chunk - 1)
        return carry

    lax.fori_loop(0, z_size, step, 0)
    multiply_both(z_size - 1, CHUNKS - 1)

    for peer in range(lay_size):
        @pl.when(peer != lay)
        def _():
            for group in range(groups):
                pltpu.make_async_remote_copy(
                    stage.at[0], landed.at[peer, group], send_lay.at[0], recv_lay.at[peer, group],
                    device_id={"lay": peer}, device_id_type=pl.DeviceIdType.MESH).wait_recv()
                own[group] = own[group] + landed[peer, group].astype(F32)
    total = jnp.concatenate([own[group] for group in range(groups)], axis=0)
    score_ref[...] = total.T

    def drain(source, carry):
        @pl.when(source // groups != lay)
        def _():
            lay_copy(source).wait_send()

        for chunk in range(CHUNKS):
            pair_copy(source, chunk, core).wait_send()
            pl.when(has_left & (source >= z))(lambda: line_copy(source, chunk, -1).wait_send())
            pl.when(has_right & (source <= z))(lambda: line_copy(source, chunk, 1).wait_send())
        return carry

    lax.fori_loop(0, z_size, drain, 0)


def solution(mesh):
    z_size, lay_size = mesh.shape["ex"] // CORES, mesh.shape["lay"]

    def on_device(train_grads, query_grads, out_basis, in_basis, eigenvalues):
        examples, width = train_grads.shape[1:]
        count = query_grads.shape[1]
        both = CORES * count
        groups = z_size // lay_size
        vmem = pl.BlockSpec(memory_space=pltpu.VMEM)
        dma = pltpu.SemaphoreType.DMA
        return pl.pallas_call(
            functools.partial(kernel, z_size, lay_size),
            out_shape=jax.ShapeDtypeStruct((examples, groups * both), F32),
            in_specs=[pl.BlockSpec(memory_space=pl.ANY), vmem, vmem, vmem, vmem],
            out_specs=vmem,
            scratch_shapes=[
                pltpu.VMEM((examples, width), BF16),
                pltpu.VMEM((z_size, CHUNKS, both, width // CHUNKS), BF16),
                pltpu.VMEM((count * width // LANES, LANES), F32),
                pltpu.VMEM((count * width // LANES, LANES), F32),
                pltpu.VMEM((2, both, examples), F32),
                pltpu.VMEM((groups, both, examples), F32),
                pltpu.VMEM((z_size, both, examples), BF16),
                pltpu.VMEM((lay_size, groups, both, examples), BF16),
                dma,
                dma((z_size, CHUNKS)),
                dma((z_size, CHUNKS)),
                dma((z_size, CHUNKS, 2)),
                dma((z_size, CHUNKS)),
                dma((z_size,)),
                dma((lay_size, groups)),
            ],
            compiler_params=pltpu.CompilerParams(
                collective_id=0, has_side_effects=True, vmem_limit_bytes=52 * 1024 * 1024
            ),
        )(train_grads, query_grads, out_basis, in_basis, eigenvalues)

    in_specs = (
        P("lay", ("grp", "ex"), None),
        P("lay", ("grp", "ex"), None),
        P("lay", None, None),
        P("lay", None, None),
        P("lay", None, None),
    )
    out_specs = P(("grp", "ex"), "lay")
    return jax.shard_map(
        on_device, mesh=mesh, in_specs=in_specs, out_specs=out_specs, check_vma=False
    )
```

```python
import functools

import jax
import jax.numpy as jnp
from jax import lax
from jax.experimental import pallas as pl
from jax.experimental.pallas import tpu as pltpu
from jax.sharding import PartitionSpec as P

DAMPING = 0.1
CORES = 2
CHUNKS = 4
LANES = 128
F32, BF16 = jnp.float32, jnp.bfloat16
NN = (((1,), (0,)), ((), ()))
NT = (((1,), (1,)), ((), ()))


def dot(a, b, dims=NN):
    return lax.dot_general(a, b, dims, preferred_element_type=F32)


def split(x):
    high = x.astype(BF16)
    return high, (x - high.astype(F32)).astype(BF16)


def kernel(z_size, lay_size, train_hbm, query_hbm, out_hbm, in_hbm, eig_hbm, score_ref,
           train, query_ref, out_ref, in_ref, eig_ref, held, by_tile, by_query, acc, own, stage, landed,
           load_sem, recv_line, recv_pair, send_line, send_pair, send_lay, recv_lay):
    ex, lay = lax.axis_index("ex"), lax.axis_index("lay")
    z, core = ex // CORES, ex % CORES
    count, width = query_ref.shape[1:]
    side = out_ref.shape[1]
    tiles = width // LANES
    columns = width // CHUNKS
    per_chunk = tiles // CHUNKS
    groups = z_size // lay_size
    has_left, has_right = z > 0, z < z_size - 1

    late = CHUNKS // 2
    first_slot, last_slot = lay == 1 // groups, lay == (z_size - 2) // groups
    send_late_left, send_late_right = (z == 1) & first_slot, (z == z_size - 2) & last_slot
    get_late_left, get_late_right = (z == z_size - 1) & last_slot, (z == 0) & first_slot

    loads = [pltpu.make_async_copy(*pair, load_sem.at[i]) for i, pair in enumerate((
        (query_hbm, query_ref), (in_hbm, in_ref), (out_hbm, out_ref), (eig_hbm, eig_ref), (train_hbm.at[0], train)))]
    for load in loads:
        load.start()

    barrier = pltpu.get_barrier_semaphore()

    def greet(target):
        pl.semaphore_signal(barrier, inc=1, device_id=target, device_id_type=pl.DeviceIdType.MESH)

    pl.when(has_left)(lambda: greet({"ex": ex - CORES}))
    pl.when(has_right)(lambda: greet({"ex": ex + CORES}))
    greet({"ex": z * CORES + 1 - core})
    for step in range(1, lay_size):
        greet({"lay": (lay + step) % lay_size})

    def line_copy(source, chunk, direction):
        block = held.at[source, chunk, pl.ds(pl.multiple_of(core * count, count), count)]
        return pltpu.make_async_remote_copy(
            block, block, send_line.at[source, chunk, (direction + 1) // 2], recv_line.at[source, chunk],
            device_id={"ex": ex + direction * CORES}, device_id_type=pl.DeviceIdType.MESH)

    def pair_copy(source, chunk, who):
        block = held.at[source, chunk, pl.ds(pl.multiple_of(who * count, count), count)]
        return pltpu.make_async_remote_copy(
            block, block, send_pair.at[source, chunk], recv_pair.at[source, chunk],
            device_id={"ex": z * CORES + 1 - core}, device_id_type=pl.DeviceIdType.MESH)

    def lay_copy(source):
        return pltpu.make_async_remote_copy(
            stage.at[source], landed.at[lay, source % groups], send_lay.at[source],
            recv_lay.at[lay, source % groups],
            device_id={"lay": source // groups}, device_id_type=pl.DeviceIdType.MESH)

    for load in loads[:-1]:
        load.wait()

    half = jnp.concatenate([in_ref[0], in_ref[0]], axis=1)
    low_lane = lax.broadcasted_iota(jnp.int32, half.shape, 1) < side
    zero = jnp.zeros_like(half)
    first, second = jnp.where(low_lane, half, 0.0), jnp.where(low_lane, 0.0, half)
    mix = jnp.concatenate([
        jnp.concatenate([first, zero], axis=1), jnp.concatenate([zero, first], axis=1),
        jnp.concatenate([second, zero], axis=1), jnp.concatenate([zero, second], axis=1)], axis=0)
    mix_high, mix_low = split(mix)
    rows = lax.broadcasted_iota(jnp.int32, (side, side), 0)
    cols = lax.broadcasted_iota(jnp.int32, (side, side), 1)
    order = (cols == 2 * (rows % tiles) + rows // tiles).astype(BF16)
    basis_high, basis_low = split(out_ref[0])
    sorted_high, sorted_low = dot(order, basis_high), dot(order, basis_low)
    to_eigen = jnp.concatenate([sorted_high.T, sorted_high.T, sorted_low.T], axis=1).astype(BF16)
    from_eigen = jnp.concatenate([sorted_high, sorted_high, sorted_low], axis=1).astype(BF16)
    scale = 1.0 / (eig_ref[0] + DAMPING)
    scale = jnp.concatenate([scale] * count, axis=1)

    for p in range(tiles):
        by_tile[p * count:(p + 1) * count, :] = query_ref[0, :, p * LANES:(p + 1) * LANES].astype(F32)

    def stacked(x):
        high, low = split(x)
        return jnp.concatenate([high, low, high], axis=0)

    pairs = jnp.concatenate([
        jnp.concatenate([by_tile[pl.ds(2 * j + i, tiles, stride=count), :] for i in range(2)], axis=1)
        for j in range(count // 2)], axis=0).astype(BF16)
    inner = dot(pairs, mix_high) + dot(pairs, mix_low)
    inner = jnp.concatenate([
        jnp.concatenate([inner[j * tiles:(j + 1) * tiles, s * LANES:(s + 1) * LANES] for s in range(2)], axis=0)
        for j in range(count // 2)], axis=1)
    rotated = dot(to_eigen, stacked(inner)) * scale
    back = dot(from_eigen, stacked(rotated))
    back = jnp.concatenate([
        jnp.concatenate([back[s * tiles:(s + 1) * tiles, j * LANES:(j + 1) * LANES] for s in range(2)], axis=1)
        for j in range(count // 2)], axis=0)
    high, low = split(back)
    result = dot(high, mix_high, NT) + dot(high, mix_low, NT) + dot(low, mix_high, NT)
    for j in range(count // 2):
        for i in range(2):
            at = (2 * j + i) * tiles
            by_query[at:at + tiles, :] = result[j * tiles:(j + 1) * tiles, i * LANES:(i + 1) * LANES]

    neighbours = has_left.astype(jnp.int32) + has_right.astype(jnp.int32) + lay_size
    pl.semaphore_wait(barrier, neighbours)

    mine = pl.ds(pl.multiple_of(core * count, count), count)
    for chunk in range(CHUNKS):
        for t in range(per_chunk):
            tile = by_query[pl.ds(chunk * per_chunk + t, count, stride=tiles), :]
            held[z, chunk, mine, t * LANES:(t + 1) * LANES] = tile.astype(BF16)
        to_left, to_right = has_left, has_right
        if chunk >= late:
            to_left, to_right = to_left & jnp.logical_not(send_late_left), to_right & jnp.logical_not(send_late_right)
        pl.when(to_left)(lambda: line_copy(z, chunk, -1).start())
        pl.when(to_right)(lambda: line_copy(z, chunk, 1).start())
        pair_copy(z, chunk, core).start()

    def send_late(direction):
        for chunk in range(late, CHUNKS):
            line_copy(z, chunk, direction).start()

    def forward(source, chunk, direction, more):
        line_copy(source, chunk, direction).wait_recv()
        if more is not False:
            pl.when(more)(lambda: line_copy(source, chunk, direction).start())
        pair_copy(source, chunk, core).start()

    def multiply(source, chunk):
        pair_copy(source, chunk, 1 - core).wait_recv()
        part = dot(held[source, chunk], train[:, chunk * columns:(chunk + 1) * columns], NT)
        if chunk > 0:
            part = part + acc[source]
        if chunk < CHUNKS - 1:
            acc[source] = part
        else:
            @pl.when(source // groups == lay)
            def _():
                own[source % groups] = part

            @pl.when(source // groups != lay)
            def _():
                stage[source] = part.astype(BF16)
                lay_copy(source).start()

    def from_right(distance, chunk):
        there = z + distance < z_size
        if chunk >= late:
            there = there & jnp.logical_not(get_late_right & (distance == 1))
        return there

    def from_left(distance, chunk):
        there = (distance >= 1) & (z - distance >= 0)
        if chunk >= late:
            there = there & jnp.logical_not(get_late_left & (distance == 1))
        return there

    def multiply_both(distance, chunk):
        pl.when((distance >= 0) & from_right(distance, chunk))(lambda: multiply(z + distance, chunk))
        pl.when(from_left(distance, chunk))(lambda: multiply(z - distance, chunk))

    loads[-1].wait()

    def step(distance, carry):
        for chunk in range(CHUNKS):
            pl.when((distance >= 1) & from_right(distance, chunk))(
                lambda: forward(z + distance, chunk, -1, has_left))
            pl.when(from_left(distance, chunk))(lambda: forward(z - distance, chunk, 1, has_right))
            if chunk == CHUNKS - 1:
                pl.when(send_late_left & (z + distance == z_size - 1))(lambda: send_late(-1))
                pl.when(send_late_right & (z - distance == 0))(lambda: send_late(1))
            if chunk == 0:
                multiply_both(distance - 1, CHUNKS - 1)
            else:
                multiply_both(distance, chunk - 1)
        return carry

    lax.fori_loop(0, z_size, step, 0)
    multiply_both(z_size - 1, CHUNKS - 1)

    def finish(source, direction):
        for chunk in range(late, CHUNKS):
            forward(source, chunk, direction, False)
        for chunk in range(late, CHUNKS):
            multiply(source, chunk)

    pl.when(get_late_right)(lambda: finish(z + 1, -1))
    pl.when(get_late_left)(lambda: finish(z - 1, 1))

    for peer in range(lay_size):
        @pl.when(peer != lay)
        def _():
            for group in range(groups):
                pltpu.make_async_remote_copy(
                    stage.at[0], landed.at[peer, group], send_lay.at[0], recv_lay.at[peer, group],
                    device_id={"lay": peer}, device_id_type=pl.DeviceIdType.MESH).wait_recv()
                own[group] = own[group] + landed[peer, group].astype(F32)
    total = jnp.concatenate([own[group] for group in range(groups)], axis=0)
    score_ref[...] = total.T

    def drain(source, carry):
        @pl.when(source // groups != lay)
        def _():
            lay_copy(source).wait_send()

        for chunk in range(CHUNKS):
            pair_copy(source, chunk, core).wait_send()
            pl.when(has_left & (source >= z))(lambda: line_copy(source, chunk, -1).wait_send())
            pl.when(has_right & (source <= z))(lambda: line_copy(source, chunk, 1).wait_send())
        return carry

    lax.fori_loop(0, z_size, drain, 0)


def solution(mesh):
    z_size, lay_size = mesh.shape["ex"] // CORES, mesh.shape["lay"]

    def on_device(train_grads, query_grads, out_basis, in_basis, eigenvalues):
        examples, width = train_grads.shape[1:]
        count = query_grads.shape[1]
        both = CORES * count
        groups = z_size // lay_size
        dma = pltpu.SemaphoreType.DMA
        return pl.pallas_call(
            functools.partial(kernel, z_size, lay_size),
            out_shape=jax.ShapeDtypeStruct((examples, groups * both), F32),
            in_specs=[pl.BlockSpec(memory_space=pl.ANY)] * 5,
            out_specs=pl.BlockSpec(memory_space=pltpu.VMEM),
            scratch_shapes=[
                pltpu.VMEM((examples, width), BF16),
                pltpu.VMEM(query_grads.shape, BF16),
                pltpu.VMEM(out_basis.shape, F32),
                pltpu.VMEM(in_basis.shape, F32),
                pltpu.VMEM(eigenvalues.shape, F32),
                pltpu.VMEM((z_size, CHUNKS, both, width // CHUNKS), BF16),
                pltpu.VMEM((count * width // LANES, LANES), F32),
                pltpu.VMEM((count * width // LANES, LANES), F32),
                pltpu.VMEM((z_size, both, examples), F32),
                pltpu.VMEM((groups, both, examples), F32),
                pltpu.VMEM((z_size, both, examples), BF16),
                pltpu.VMEM((lay_size, groups, both, examples), BF16),
                dma((5,)),
                dma((z_size, CHUNKS)),
                dma((z_size, CHUNKS)),
                dma((z_size, CHUNKS, 2)),
                dma((z_size, CHUNKS)),
                dma((z_size,)),
                dma((lay_size, groups)),
            ],
            compiler_params=pltpu.CompilerParams(
                collective_id=0, has_side_effects=True, vmem_limit_bytes=60 * 1024 * 1024
            ),
        )(train_grads, query_grads, out_basis, in_basis, eigenvalues)

    in_specs = (
        P("lay", ("grp", "ex"), None),
        P("lay", ("grp", "ex"), None),
        P("lay", None, None),
        P("lay", None, None),
        P("lay", None, None),
    )
    out_specs = P(("grp", "ex"), "lay")
    return jax.shard_map(
        on_device, mesh=mesh, in_specs=in_specs, out_specs=out_specs, check_vma=False
    )
```

```python
import functools

import jax
import jax.numpy as jnp
from jax import lax
from jax.experimental import pallas as pl
from jax.experimental.pallas import tpu as pltpu
from jax.sharding import PartitionSpec as P

DAMPING = 0.1
CORES = 2
CHUNKS = 4
LANES = 128
F32, BF16 = jnp.float32, jnp.bfloat16
NN = (((1,), (0,)), ((), ()))
NT = (((1,), (1,)), ((), ()))


def dot(a, b, dims=NN):
    return lax.dot_general(a, b, dims, preferred_element_type=F32)


def split(x):
    high = x.astype(BF16)
    return high, (x - high.astype(F32)).astype(BF16)


def kernel(z_size, lay_size, train_hbm, query_hbm, out_hbm, in_hbm, eig_hbm, score_ref,
           train, query_ref, out_ref, in_ref, eig_ref, held, by_tile, by_query, acc, own, stage, landed,
           load_sem, recv_line, recv_pair, send_line, send_pair, send_lay, recv_lay):
    ex, lay = lax.axis_index("ex"), lax.axis_index("lay")
    z, core = ex // CORES, ex % CORES
    count, width = query_ref.shape[1:]
    side = out_ref.shape[1]
    tiles = width // LANES
    columns = width // CHUNKS
    per_chunk = tiles // CHUNKS
    groups = z_size // lay_size
    has_left, has_right = z > 0, z < z_size - 1

    late = CHUNKS - 1
    first_slot, last_slot = lay == 1 // groups, lay == (z_size - 2) // groups
    send_late_left, send_late_right = (z == 1) & first_slot, (z == z_size - 2) & last_slot
    get_late_left, get_late_right = (z == z_size - 1) & last_slot, (z == 0) & first_slot

    loads = [pltpu.make_async_copy(*pair, load_sem.at[i]) for i, pair in enumerate((
        (query_hbm, query_ref), (in_hbm, in_ref), (out_hbm, out_ref), (eig_hbm, eig_ref), (train_hbm.at[0], train)))]
    for load in loads:
        load.start()

    barrier = pltpu.get_barrier_semaphore()

    def greet(target):
        pl.semaphore_signal(barrier, inc=1, device_id=target, device_id_type=pl.DeviceIdType.MESH)

    pl.when(has_left)(lambda: greet({"ex": ex - CORES}))
    pl.when(has_right)(lambda: greet({"ex": ex + CORES}))
    greet({"ex": z * CORES + 1 - core})
    for step in range(1, lay_size):
        greet({"lay": (lay + step) % lay_size})

    def line_copy(source, chunk, direction):
        block = held.at[source, chunk, pl.ds(pl.multiple_of(core * count, count), count)]
        return pltpu.make_async_remote_copy(
            block, block, send_line.at[source, chunk, (direction + 1) // 2], recv_line.at[source, chunk],
            device_id={"ex": ex + direction * CORES}, device_id_type=pl.DeviceIdType.MESH)

    def pair_copy(source, chunk, who):
        block = held.at[source, chunk, pl.ds(pl.multiple_of(who * count, count), count)]
        return pltpu.make_async_remote_copy(
            block, block, send_pair.at[source, chunk], recv_pair.at[source, chunk],
            device_id={"ex": z * CORES + 1 - core}, device_id_type=pl.DeviceIdType.MESH)

    def lay_copy(source):
        return pltpu.make_async_remote_copy(
            stage.at[source], landed.at[lay, source % groups], send_lay.at[source],
            recv_lay.at[lay, source % groups],
            device_id={"lay": source // groups}, device_id_type=pl.DeviceIdType.MESH)

    for load in loads[:-1]:
        load.wait()

    half = jnp.concatenate([in_ref[0], in_ref[0]], axis=1)
    low_lane = lax.broadcasted_iota(jnp.int32, half.shape, 1) < side
    zero = jnp.zeros_like(half)
    first, second = jnp.where(low_lane, half, 0.0), jnp.where(low_lane, 0.0, half)
    mix = jnp.concatenate([
        jnp.concatenate([first, zero], axis=1), jnp.concatenate([zero, first], axis=1),
        jnp.concatenate([second, zero], axis=1), jnp.concatenate([zero, second], axis=1)], axis=0)
    mix_high, mix_low = split(mix)
    rows = lax.broadcasted_iota(jnp.int32, (side, side), 0)
    cols = lax.broadcasted_iota(jnp.int32, (side, side), 1)
    order = (cols == 2 * (rows % tiles) + rows // tiles).astype(BF16)
    basis_high, basis_low = split(out_ref[0])
    sorted_high, sorted_low = dot(order, basis_high), dot(order, basis_low)
    to_eigen = jnp.concatenate([sorted_high.T, sorted_high.T, sorted_low.T], axis=1).astype(BF16)
    from_eigen = jnp.concatenate([sorted_high, sorted_high, sorted_low], axis=1).astype(BF16)
    scale = 1.0 / (eig_ref[0] + DAMPING)
    scale = jnp.concatenate([scale] * count, axis=1)

    for p in range(tiles):
        by_tile[p * count:(p + 1) * count, :] = query_ref[0, :, p * LANES:(p + 1) * LANES].astype(F32)

    def stacked(x):
        high, low = split(x)
        return jnp.concatenate([high, low, high], axis=0)

    pairs = jnp.concatenate([
        jnp.concatenate([by_tile[pl.ds(2 * j + i, tiles, stride=count), :] for i in range(2)], axis=1)
        for j in range(count // 2)], axis=0).astype(BF16)
    inner = dot(pairs, mix_high) + dot(pairs, mix_low)
    inner = jnp.concatenate([
        jnp.concatenate([inner[j * tiles:(j + 1) * tiles, s * LANES:(s + 1) * LANES] for s in range(2)], axis=0)
        for j in range(count // 2)], axis=1)
    rotated = dot(to_eigen, stacked(inner)) * scale
    back = dot(from_eigen, stacked(rotated))
    back = jnp.concatenate([
        jnp.concatenate([back[s * tiles:(s + 1) * tiles, j * LANES:(j + 1) * LANES] for s in range(2)], axis=1)
        for j in range(count // 2)], axis=0)
    high, low = split(back)
    result = dot(high, mix_high, NT) + dot(high, mix_low, NT) + dot(low, mix_high, NT)
    for j in range(count // 2):
        for i in range(2):
            at = (2 * j + i) * tiles
            by_query[at:at + tiles, :] = result[j * tiles:(j + 1) * tiles, i * LANES:(i + 1) * LANES]

    neighbours = has_left.astype(jnp.int32) + has_right.astype(jnp.int32) + lay_size
    pl.semaphore_wait(barrier, neighbours)

    mine = pl.ds(pl.multiple_of(core * count, count), count)
    for chunk in range(CHUNKS):
        for t in range(per_chunk):
            tile = by_query[pl.ds(chunk * per_chunk + t, count, stride=tiles), :]
            held[z, chunk, mine, t * LANES:(t + 1) * LANES] = tile.astype(BF16)
        to_left, to_right = has_left, has_right
        if chunk >= late:
            to_left, to_right = to_left & jnp.logical_not(send_late_left), to_right & jnp.logical_not(send_late_right)
        pl.when(to_left)(lambda: line_copy(z, chunk, -1).start())
        pl.when(to_right)(lambda: line_copy(z, chunk, 1).start())
        pair_copy(z, chunk, core).start()

    def send_late(direction):
        for chunk in range(late, CHUNKS):
            line_copy(z, chunk, direction).start()

    def forward(source, chunk, direction, more):
        line_copy(source, chunk, direction).wait_recv()
        if more is not False:
            pl.when(more)(lambda: line_copy(source, chunk, direction).start())
        pair_copy(source, chunk, core).start()

    def multiply(source, chunk):
        pair_copy(source, chunk, 1 - core).wait_recv()
        part = dot(held[source, chunk], train[:, chunk * columns:(chunk + 1) * columns], NT)
        if chunk > 0:
            part = part + acc[source]
        if chunk < CHUNKS - 1:
            acc[source] = part
        else:
            @pl.when(source // groups == lay)
            def _():
                own[source % groups] = part

            @pl.when(source // groups != lay)
            def _():
                stage[source] = part.astype(BF16)
                lay_copy(source).start()

    def from_right(distance, chunk):
        there = z + distance < z_size
        if chunk >= late:
            there = there & jnp.logical_not(get_late_right & (distance == 1))
        return there

    def from_left(distance, chunk):
        there = (distance >= 1) & (z - distance >= 0)
        if chunk >= late:
            there = there & jnp.logical_not(get_late_left & (distance == 1))
        return there

    def multiply_both(distance, chunk):
        pl.when((distance >= 0) & from_right(distance, chunk))(lambda: multiply(z + distance, chunk))
        pl.when(from_left(distance, chunk))(lambda: multiply(z - distance, chunk))

    loads[-1].wait()

    def step(distance, carry):
        for chunk in range(CHUNKS):
            pl.when((distance >= 1) & from_right(distance, chunk))(
                lambda: forward(z + distance, chunk, -1, has_left))
            pl.when(from_left(distance, chunk))(lambda: forward(z - distance, chunk, 1, has_right))
            if chunk == CHUNKS - 1:
                pl.when(send_late_left & (z + distance == z_size - 1))(lambda: send_late(-1))
                pl.when(send_late_right & (z - distance == 0))(lambda: send_late(1))
            if chunk == 0:
                multiply_both(distance - 1, CHUNKS - 1)
            else:
                multiply_both(distance, chunk - 1)
        return carry

    lax.fori_loop(0, z_size, step, 0)
    multiply_both(z_size - 1, CHUNKS - 1)

    def finish(source, direction):
        for chunk in range(late, CHUNKS):
            forward(source, chunk, direction, False)
        for chunk in range(late, CHUNKS):
            multiply(source, chunk)

    pl.when(get_late_right)(lambda: finish(z + 1, -1))
    pl.when(get_late_left)(lambda: finish(z - 1, 1))

    for peer in range(lay_size):
        @pl.when(peer != lay)
        def _():
            for group in range(groups):
                pltpu.make_async_remote_copy(
                    stage.at[0], landed.at[peer, group], send_lay.at[0], recv_lay.at[peer, group],
                    device_id={"lay": peer}, device_id_type=pl.DeviceIdType.MESH).wait_recv()
                own[group] = own[group] + landed[peer, group].astype(F32)
    total = jnp.concatenate([own[group] for group in range(groups)], axis=0)
    score_ref[...] = total.T

    def drain(source, carry):
        @pl.when(source // groups != lay)
        def _():
            lay_copy(source).wait_send()

        for chunk in range(CHUNKS):
            pair_copy(source, chunk, core).wait_send()
            pl.when(has_left & (source >= z))(lambda: line_copy(source, chunk, -1).wait_send())
            pl.when(has_right & (source <= z))(lambda: line_copy(source, chunk, 1).wait_send())
        return carry

    lax.fori_loop(0, z_size, drain, 0)


def solution(mesh):
    z_size, lay_size = mesh.shape["ex"] // CORES, mesh.shape["lay"]

    def on_device(train_grads, query_grads, out_basis, in_basis, eigenvalues):
        examples, width = train_grads.shape[1:]
        count = query_grads.shape[1]
        both = CORES * count
        groups = z_size // lay_size
        dma = pltpu.SemaphoreType.DMA
        return pl.pallas_call(
            functools.partial(kernel, z_size, lay_size),
            out_shape=pltpu.VMEM((examples, groups * both), F32),
            in_specs=[pl.BlockSpec(memory_space=pl.ANY)] * 5,
            out_specs=pl.BlockSpec(memory_space=pltpu.VMEM),
            scratch_shapes=[
                pltpu.VMEM((examples, width), BF16),
                pltpu.VMEM(query_grads.shape, BF16),
                pltpu.VMEM(out_basis.shape, F32),
                pltpu.VMEM(in_basis.shape, F32),
                pltpu.VMEM(eigenvalues.shape, F32),
                pltpu.VMEM((z_size, CHUNKS, both, width // CHUNKS), BF16),
                pltpu.VMEM((count * width // LANES, LANES), F32),
                pltpu.VMEM((count * width // LANES, LANES), F32),
                pltpu.VMEM((z_size, both, examples), F32),
                pltpu.VMEM((groups, both, examples), F32),
                pltpu.VMEM((z_size, both, examples), BF16),
                pltpu.VMEM((lay_size, groups, both, examples), BF16),
                dma((5,)),
                dma((z_size, CHUNKS)),
                dma((z_size, CHUNKS)),
                dma((z_size, CHUNKS, 2)),
                dma((z_size, CHUNKS)),
                dma((z_size,)),
                dma((lay_size, groups)),
            ],
            compiler_params=pltpu.CompilerParams(
                collective_id=0, has_side_effects=True, vmem_limit_bytes=58 * 1024 * 1024
            ),
        )(train_grads, query_grads, out_basis, in_basis, eigenvalues)

    in_specs = (
        P("lay", ("grp", "ex"), None),
        P("lay", ("grp", "ex"), None),
        P("lay", None, None),
        P("lay", None, None),
        P("lay", None, None),
    )
    out_specs = P(("grp", "ex"), "lay")
    return jax.shard_map(
        on_device, mesh=mesh, in_specs=in_specs, out_specs=out_specs, check_vma=False
    )
```

```python
import functools

import jax
import jax.numpy as jnp
from jax import lax
from jax.experimental import pallas as pl
from jax.experimental.pallas import tpu as pltpu
from jax.sharding import PartitionSpec as P

DAMPING = 0.1
CORES = 2
CHUNKS = 4
LANES = 128
F32, BF16 = jnp.float32, jnp.bfloat16
NN = (((1,), (0,)), ((), ()))
NT = (((1,), (1,)), ((), ()))


def dot(a, b, dims=NN):
    return lax.dot_general(a, b, dims, preferred_element_type=F32)


def split(x):
    high = x.astype(BF16)
    return high, (x - high.astype(F32)).astype(BF16)


def kernel(z_size, lay_size, train_hbm, query_hbm, out_hbm, in_hbm, eig_hbm, score_ref,
           train, query_ref, out_ref, in_ref, eig_ref, raw, held, mix_ref, to_ref, from_ref, scale_ref,
           by_tile, by_query, acc, own, stage, landed,
           load_sem, recv_line, recv_pair, send_line, send_pair, send_lay, recv_lay):
    ex, lay = lax.axis_index("ex"), lax.axis_index("lay")
    z, core = ex // CORES, ex % CORES
    count, width = query_ref.shape[1:]
    side = out_ref.shape[1]
    tiles = width // LANES
    part_rows = count // 2
    columns = width // 2
    per_chunk = tiles // 2
    groups = z_size // lay_size
    has_left, has_right = z > 0, z < z_size - 1

    late = CHUNKS - 1
    first_slot, last_slot = lay == 1 // groups, lay == (z_size - 2) // groups
    send_late_left, send_late_right = (z == 1) & first_slot, (z == z_size - 2) & last_slot
    get_late_left, get_late_right = (z == z_size - 1) & last_slot, (z == 0) & first_slot

    loads = [pltpu.make_async_copy(*pair, load_sem.at[i]) for i, pair in enumerate((
        (query_hbm, query_ref), (in_hbm, in_ref), (out_hbm, out_ref), (eig_hbm, eig_ref), (train_hbm.at[0], train)))]
    for load in loads:
        load.start()

    barrier = pltpu.get_barrier_semaphore()

    def greet(target):
        pl.semaphore_signal(barrier, inc=1, device_id=target, device_id_type=pl.DeviceIdType.MESH)

    pl.when(has_left)(lambda: greet({"ex": ex - CORES}))
    pl.when(has_right)(lambda: greet({"ex": ex + CORES}))
    greet({"ex": z * CORES + 1 - core})
    for step in range(1, lay_size):
        greet({"lay": (lay + step) % lay_size})

    mine = pl.ds(pl.multiple_of(core * part_rows, part_rows), part_rows)

    def line_copy(source, chunk, direction, own_raw=False):
        block = raw.at[source, chunk] if chunk < 2 else held.at[source, chunk, mine]
        start = query_hbm.at[0, pl.ds(0, part_rows), pl.ds(chunk * columns, columns)] if own_raw else block
        return pltpu.make_async_remote_copy(
            start, block, send_line.at[source, chunk, (direction + 1) // 2], recv_line.at[source, chunk],
            device_id={"ex": ex + direction * CORES}, device_id_type=pl.DeviceIdType.MESH)

    def pair_copy(source, chunk, who):
        block = held.at[source, chunk, pl.ds(pl.multiple_of(who * part_rows, part_rows), part_rows)]
        return pltpu.make_async_remote_copy(
            block, block, send_pair.at[source, chunk], recv_pair.at[source, chunk],
            device_id={"ex": z * CORES + 1 - core}, device_id_type=pl.DeviceIdType.MESH)

    def lay_copy(source):
        return pltpu.make_async_remote_copy(
            stage.at[source], landed.at[lay, source % groups], send_lay.at[source],
            recv_lay.at[lay, source % groups],
            device_id={"lay": source // groups}, device_id_type=pl.DeviceIdType.MESH)

    neighbours = has_left.astype(jnp.int32) + has_right.astype(jnp.int32) + lay_size
    pl.semaphore_wait(barrier, neighbours)
    for chunk in range(2):
        pl.when(has_left)(lambda: line_copy(z, chunk, -1, True).start())
        pl.when(has_right)(lambda: line_copy(z, chunk, 1, True).start())

    for load in loads[:-1]:
        load.wait()

    half = jnp.concatenate([in_ref[0], in_ref[0]], axis=1)
    low_lane = lax.broadcasted_iota(jnp.int32, half.shape, 1) < side
    zero = jnp.zeros_like(half)
    first, second = jnp.where(low_lane, half, 0.0), jnp.where(low_lane, 0.0, half)
    mix = jnp.concatenate([
        jnp.concatenate([first, zero], axis=1), jnp.concatenate([zero, first], axis=1),
        jnp.concatenate([second, zero], axis=1), jnp.concatenate([zero, second], axis=1)], axis=0)
    mix_high, mix_low = split(mix)
    rows = lax.broadcasted_iota(jnp.int32, (side, side), 0)
    cols = lax.broadcasted_iota(jnp.int32, (side, side), 1)
    order = (cols == 2 * (rows % tiles) + rows // tiles).astype(BF16)
    basis_high, basis_low = split(out_ref[0])
    sorted_high, sorted_low = dot(order, basis_high), dot(order, basis_low)
    to_eigen = jnp.concatenate([sorted_high.T, sorted_high.T, sorted_low.T], axis=1).astype(BF16)
    from_eigen = jnp.concatenate([sorted_high, sorted_high, sorted_low], axis=1).astype(BF16)
    scale = 1.0 / (eig_ref[0] + DAMPING)
    mix_ref[0], mix_ref[1] = mix_high, mix_low
    to_ref[...], from_ref[...] = to_eigen, from_eigen
    scale_ref[...] = jnp.concatenate([scale] * part_rows, axis=1)

    def stacked(x):
        high, low = split(x)
        return jnp.concatenate([high, low, high], axis=0)

    def precondition(source, first_chunk, tile_of):
        for p in range(tiles):
            by_tile[p * part_rows:(p + 1) * part_rows, :] = tile_of(p).astype(F32)
        pairs = jnp.concatenate([
            jnp.concatenate([by_tile[pl.ds(2 * j + i, tiles, stride=part_rows), :] for i in range(2)], axis=1)
            for j in range(part_rows // 2)], axis=0).astype(BF16)
        inner = dot(pairs, mix_ref[0]) + dot(pairs, mix_ref[1])
        inner = jnp.concatenate([
            jnp.concatenate([inner[j * tiles:(j + 1) * tiles, s * LANES:(s + 1) * LANES] for s in range(2)], axis=0)
            for j in range(part_rows // 2)], axis=1)
        rotated = dot(to_ref[...], stacked(inner)) * scale_ref[...]
        back = dot(from_ref[...], stacked(rotated))
        back = jnp.concatenate([
            jnp.concatenate([back[s * tiles:(s + 1) * tiles, j * LANES:(j + 1) * LANES] for s in range(2)], axis=1)
            for j in range(part_rows // 2)], axis=0)
        high, low = split(back)
        result = dot(high, mix_ref[0], NT) + dot(high, mix_ref[1], NT) + dot(low, mix_ref[0], NT)
        for j in range(part_rows // 2):
            for i in range(2):
                at = (2 * j + i) * tiles
                by_query[at:at + tiles, :] = result[j * tiles:(j + 1) * tiles, i * LANES:(i + 1) * LANES]
        for chunk in range(2):
            for t in range(per_chunk):
                tile = by_query[pl.ds(chunk * per_chunk + t, part_rows, stride=tiles), :]
                held[source, first_chunk + chunk, mine, t * LANES:(t + 1) * LANES] = tile.astype(BF16)

    precondition(z, 2, lambda p: query_ref[0, part_rows:, p * LANES:(p + 1) * LANES])
    for chunk in range(2, CHUNKS):
        to_left, to_right = has_left, has_right
        if chunk >= late:
            to_left, to_right = to_left & jnp.logical_not(send_late_left), to_right & jnp.logical_not(send_late_right)
        pl.when(to_left)(lambda: line_copy(z, chunk, -1).start())
        pl.when(to_right)(lambda: line_copy(z, chunk, 1).start())
        pair_copy(z, chunk, core).start()
    precondition(z, 0, lambda p: query_ref[0, :part_rows, p * LANES:(p + 1) * LANES])
    for chunk in range(2):
        pair_copy(z, chunk, core).start()

    def send_late(direction):
        for chunk in range(late, CHUNKS):
            line_copy(z, chunk, direction).start()

    def forward(source, chunk, direction, more):
        line_copy(source, chunk, direction).wait_recv()
        if more is not False:
            pl.when(more)(lambda: line_copy(source, chunk, direction).start())
        if chunk >= 2:
            pair_copy(source, chunk, core).start()
        elif chunk == 1:
            precondition(source, 0, lambda p: raw[
                source, p // per_chunk, :, p % per_chunk * LANES:(p % per_chunk + 1) * LANES])
            for done in range(2):
                pair_copy(source, done, core).start()

    def multiply(source, chunk):
        pair_copy(source, chunk, 1 - core).wait_recv()
        column, half = chunk % 2, chunk // 2
        part = dot(held[source, chunk], train[:, column * columns:(column + 1) * columns], NT)
        if column == 0:
            acc[source] = part
        else:
            part = part + acc[source]
            pieces = [(slice(who * count + half * part_rows, who * count + (half + 1) * part_rows),
                       part[who * part_rows:(who + 1) * part_rows]) for who in range(CORES)]

            @pl.when(source // groups == lay)
            def _():
                for at, piece in pieces:
                    own[source % groups, at] = piece

            @pl.when(source // groups != lay)
            def _():
                for at, piece in pieces:
                    stage[source, at] = piece.astype(BF16)
                if half == 1:
                    lay_copy(source).start()

    def from_right(distance, chunk):
        there = z + distance < z_size
        if chunk >= late:
            there = there & jnp.logical_not(get_late_right & (distance == 1))
        return there

    def from_left(distance, chunk):
        there = (distance >= 1) & (z - distance >= 0)
        if chunk >= late:
            there = there & jnp.logical_not(get_late_left & (distance == 1))
        return there

    def multiply_both(distance, chunk, also=True):
        pl.when(also & (distance >= 0) & from_right(distance, chunk))(lambda: multiply(z + distance, chunk))
        pl.when(also & from_left(distance, chunk))(lambda: multiply(z - distance, chunk))

    loads[-1].wait()

    def step(distance, carry):
        for chunk in range(CHUNKS):
            pl.when((distance >= 1) & from_right(distance, chunk))(
                lambda: forward(z + distance, chunk, -1, has_left))
            pl.when(from_left(distance, chunk))(lambda: forward(z - distance, chunk, 1, has_right))
            if chunk == CHUNKS - 1:
                pl.when(send_late_left & (z + distance == z_size - 1))(lambda: send_late(-1))
                pl.when(send_late_right & (z - distance == 0))(lambda: send_late(1))
            if chunk == 0:
                multiply_both(distance - 1, 3)
            elif chunk == 2:
                multiply_both(distance, 0)
                multiply_both(distance, 1, distance != 1)
            elif chunk == 3:
                multiply_both(distance, 1, distance == 1)
                multiply_both(distance, 2)
        return carry

    lax.fori_loop(0, z_size, step, 0)
    multiply_both(z_size - 1, CHUNKS - 1)

    def finish(source, direction):
        for chunk in range(late, CHUNKS):
            forward(source, chunk, direction, False)
        for chunk in range(late, CHUNKS):
            multiply(source, chunk)

    pl.when(get_late_right)(lambda: finish(z + 1, -1))
    pl.when(get_late_left)(lambda: finish(z - 1, 1))

    for peer in range(lay_size):
        @pl.when(peer != lay)
        def _():
            for group in range(groups):
                pltpu.make_async_remote_copy(
                    stage.at[0], landed.at[peer, group], send_lay.at[0], recv_lay.at[peer, group],
                    device_id={"lay": peer}, device_id_type=pl.DeviceIdType.MESH).wait_recv()
                own[group] = own[group] + landed[peer, group].astype(F32)
    total = jnp.concatenate([own[group] for group in range(groups)], axis=0)
    score_ref[...] = total.T

    def drain(source, carry):
        @pl.when(source // groups != lay)
        def _():
            lay_copy(source).wait_send()

        for chunk in range(CHUNKS):
            pair_copy(source, chunk, core).wait_send()
            pl.when(has_left & (source >= z))(lambda: line_copy(source, chunk, -1).wait_send())
            pl.when(has_right & (source <= z))(lambda: line_copy(source, chunk, 1).wait_send())
        return carry

    lax.fori_loop(0, z_size, drain, 0)


def solution(mesh):
    z_size, lay_size = mesh.shape["ex"] // CORES, mesh.shape["lay"]

    def on_device(train_grads, query_grads, out_basis, in_basis, eigenvalues):
        examples, width = train_grads.shape[1:]
        count = query_grads.shape[1]
        both = CORES * count
        groups = z_size // lay_size
        side = out_basis.shape[1]
        dma = pltpu.SemaphoreType.DMA
        return pl.pallas_call(
            functools.partial(kernel, z_size, lay_size),
            out_shape=pltpu.VMEM((examples, groups * both), F32),
            in_specs=[pl.BlockSpec(memory_space=pl.ANY)] * 5,
            out_specs=pl.BlockSpec(memory_space=pltpu.VMEM),
            scratch_shapes=[
                pltpu.VMEM((examples, width), BF16),
                pltpu.VMEM(query_grads.shape, BF16),
                pltpu.VMEM(out_basis.shape, F32),
                pltpu.VMEM(in_basis.shape, F32),
                pltpu.VMEM(eigenvalues.shape, F32),
                pltpu.VMEM((z_size, 2, count // 2, width // 2), BF16),
                pltpu.VMEM((z_size, CHUNKS, count, width // 2), BF16),
                pltpu.VMEM((2, 2 * LANES, 2 * LANES), BF16),
                pltpu.VMEM((side, 3 * side), BF16),
                pltpu.VMEM((side, 3 * side), BF16),
                pltpu.VMEM((side, count // 2 * side), F32),
                pltpu.VMEM((count * width // 2 // LANES, LANES), F32),
                pltpu.VMEM((count * width // 2 // LANES, LANES), F32),
                pltpu.VMEM((z_size, count, examples), F32),
                pltpu.VMEM((groups, both, examples), F32),
                pltpu.VMEM((z_size, both, examples), BF16),
                pltpu.VMEM((lay_size, groups, both, examples), BF16),
                dma((5,)),
                dma((z_size, CHUNKS)),
                dma((z_size, CHUNKS)),
                dma((z_size, CHUNKS, 2)),
                dma((z_size, CHUNKS)),
                dma((z_size,)),
                dma((lay_size, groups)),
            ],
            compiler_params=pltpu.CompilerParams(
                collective_id=0, has_side_effects=True, vmem_limit_bytes=58 * 1024 * 1024
            ),
        )(train_grads, query_grads, out_basis, in_basis, eigenvalues)

    in_specs = (
        P("lay", ("grp", "ex"), None),
        P("lay", ("grp", "ex"), None),
        P("lay", None, None),
        P("lay", None, None),
        P("lay", None, None),
    )
    out_specs = P(("grp", "ex"), "lay")
    return jax.shard_map(
        on_device, mesh=mesh, in_specs=in_specs, out_specs=out_specs, check_vma=False
    )
```

```python
import functools

import jax
import jax.numpy as jnp
from jax import lax
from jax.experimental import pallas as pl
from jax.experimental.pallas import tpu as pltpu
from jax.sharding import PartitionSpec as P

DAMPING = 0.1
CORES = 2
CHUNKS = 4
LANES = 128
F32, BF16 = jnp.float32, jnp.bfloat16
NN = (((1,), (0,)), ((), ()))
NT = (((1,), (1,)), ((), ()))


def dot(a, b, dims=NN):
    return lax.dot_general(a, b, dims, preferred_element_type=F32)


def split(x):
    high = x.astype(BF16)
    return high, (x - high.astype(F32)).astype(BF16)


def kernel(z_size, lay_size, train_hbm, query_hbm, out_hbm, in_hbm, eig_hbm, score_ref,
           train, query_ref, out_ref, in_ref, eig_ref, raw, held, mix_ref, to_ref, from_ref, scale_ref,
           by_tile, by_query, acc, own, stage, landed,
           load_sem, recv_line, recv_pair, send_line, send_pair, send_lay, recv_lay):
    ex, lay = lax.axis_index("ex"), lax.axis_index("lay")
    z, core = ex // CORES, ex % CORES
    count, width = query_ref.shape[1:]
    side = out_ref.shape[1]
    tiles = width // LANES
    part_rows = count // 2
    columns = width // 2
    per_chunk = tiles // 2
    groups = z_size // lay_size
    has_left, has_right = z > 0, z < z_size - 1

    late = CHUNKS - 1
    first_slot, last_slot = lay == 1 // groups, lay == (z_size - 2) // groups
    send_late_left, send_late_right = (z == 1) & first_slot, (z == z_size - 2) & last_slot
    get_late_left, get_late_right = (z == z_size - 1) & last_slot, (z == 0) & first_slot

    loads = [pltpu.make_async_copy(*pair, load_sem.at[i]) for i, pair in enumerate((
        (query_hbm, query_ref), (in_hbm, in_ref), (out_hbm, out_ref), (eig_hbm, eig_ref), (train_hbm.at[0], train)))]
    for load in loads:
        load.start()

    barrier = pltpu.get_barrier_semaphore()

    def greet(target):
        pl.semaphore_signal(barrier, inc=1, device_id=target, device_id_type=pl.DeviceIdType.MESH)

    pl.when(has_left)(lambda: greet({"ex": ex - CORES}))
    pl.when(has_right)(lambda: greet({"ex": ex + CORES}))
    greet({"ex": z * CORES + 1 - core})
    for step in range(1, lay_size):
        greet({"lay": (lay + step) % lay_size})

    mine = pl.ds(pl.multiple_of(core * part_rows, part_rows), part_rows)

    def line_copy(source, chunk, direction, own_raw=False):
        block = raw.at[source, chunk] if chunk < 2 else held.at[source, chunk, mine]
        start = query_hbm.at[0, pl.ds(0, part_rows), pl.ds(chunk * columns, columns)] if own_raw else block
        return pltpu.make_async_remote_copy(
            start, block, send_line.at[source, chunk, (direction + 1) // 2], recv_line.at[source, chunk],
            device_id={"ex": ex + direction * CORES}, device_id_type=pl.DeviceIdType.MESH)

    def pair_copy(source, chunk, who):
        block = held.at[source, chunk, pl.ds(pl.multiple_of(who * part_rows, part_rows), part_rows)]
        return pltpu.make_async_remote_copy(
            block, block, send_pair.at[source, chunk], recv_pair.at[source, chunk],
            device_id={"ex": z * CORES + 1 - core}, device_id_type=pl.DeviceIdType.MESH)

    def lay_copy(source):
        return pltpu.make_async_remote_copy(
            stage.at[source], landed.at[lay, source % groups], send_lay.at[source],
            recv_lay.at[lay, source % groups],
            device_id={"lay": source // groups}, device_id_type=pl.DeviceIdType.MESH)

    neighbours = has_left.astype(jnp.int32) + has_right.astype(jnp.int32) + lay_size
    pl.semaphore_wait(barrier, neighbours)
    for chunk in range(2):
        pl.when(has_left)(lambda: line_copy(z, chunk, -1, True).start())
        pl.when(has_right)(lambda: line_copy(z, chunk, 1, True).start())

    for load in loads[:-1]:
        load.wait()

    half = jnp.concatenate([in_ref[0], in_ref[0]], axis=1)
    low_lane = lax.broadcasted_iota(jnp.int32, half.shape, 1) < side
    zero = jnp.zeros_like(half)
    first, second = jnp.where(low_lane, half, 0.0), jnp.where(low_lane, 0.0, half)
    mix = jnp.concatenate([
        jnp.concatenate([first, zero], axis=1), jnp.concatenate([zero, first], axis=1),
        jnp.concatenate([second, zero], axis=1), jnp.concatenate([zero, second], axis=1)], axis=0)
    mix_high, mix_low = split(mix)
    rows = lax.broadcasted_iota(jnp.int32, (side, side), 0)
    cols = lax.broadcasted_iota(jnp.int32, (side, side), 1)
    order = (cols == 2 * (rows % tiles) + rows // tiles).astype(BF16)
    basis_high, basis_low = split(out_ref[0])
    sorted_high, sorted_low = dot(order, basis_high), dot(order, basis_low)
    to_eigen = jnp.concatenate([sorted_high.T, sorted_high.T, sorted_low.T], axis=1).astype(BF16)
    from_eigen = jnp.concatenate([sorted_high, sorted_high, sorted_low], axis=1).astype(BF16)
    scale = 1.0 / (eig_ref[0] + DAMPING)
    mix_ref[0], mix_ref[1] = mix_high, mix_low
    to_ref[...], from_ref[...] = to_eigen, from_eigen
    scale_ref[...] = jnp.concatenate([scale] * part_rows, axis=1)

    def stacked(x):
        high, low = split(x)
        return jnp.concatenate([high, low, high], axis=0)

    def precondition(source, first_chunk, tile_of):
        for p in range(tiles):
            by_tile[p * part_rows:(p + 1) * part_rows, :] = tile_of(p).astype(F32)
        pairs = jnp.concatenate([
            jnp.concatenate([by_tile[pl.ds(2 * j + i, tiles, stride=part_rows), :] for i in range(2)], axis=1)
            for j in range(part_rows // 2)], axis=0).astype(BF16)
        inner = dot(pairs, mix_ref[0]) + dot(pairs, mix_ref[1])
        inner = jnp.concatenate([
            jnp.concatenate([inner[j * tiles:(j + 1) * tiles, s * LANES:(s + 1) * LANES] for s in range(2)], axis=0)
            for j in range(part_rows // 2)], axis=1)
        rotated = dot(to_ref[...], stacked(inner)) * scale_ref[...]
        back = dot(from_ref[...], stacked(rotated))
        back = jnp.concatenate([
            jnp.concatenate([back[s * tiles:(s + 1) * tiles, j * LANES:(j + 1) * LANES] for s in range(2)], axis=1)
            for j in range(part_rows // 2)], axis=0)
        high, low = split(back)
        result = dot(high, mix_ref[0], NT) + dot(high, mix_ref[1], NT) + dot(low, mix_ref[0], NT)
        for j in range(part_rows // 2):
            for i in range(2):
                at = (2 * j + i) * tiles
                by_query[at:at + tiles, :] = result[j * tiles:(j + 1) * tiles, i * LANES:(i + 1) * LANES]
        for chunk in range(2):
            for t in range(per_chunk):
                tile = by_query[pl.ds(chunk * per_chunk + t, part_rows, stride=tiles), :]
                held[source, first_chunk + chunk, mine, t * LANES:(t + 1) * LANES] = tile.astype(BF16)

    precondition(z, 2, lambda p: query_ref[0, part_rows:, p * LANES:(p + 1) * LANES])
    for chunk in range(2, CHUNKS):
        to_left, to_right = has_left, has_right
        if chunk >= late:
            to_left, to_right = to_left & jnp.logical_not(send_late_left), to_right & jnp.logical_not(send_late_right)
        pl.when(to_left)(lambda: line_copy(z, chunk, -1).start())
        pl.when(to_right)(lambda: line_copy(z, chunk, 1).start())
        pair_copy(z, chunk, core).start()
    precondition(z, 0, lambda p: query_ref[0, :part_rows, p * LANES:(p + 1) * LANES])
    for chunk in range(2):
        pair_copy(z, chunk, core).start()

    def send_late(direction):
        for chunk in range(late, CHUNKS):
            line_copy(z, chunk, direction).start()

    def forward(source, chunk, direction, more):
        line_copy(source, chunk, direction).wait_recv()
        if more is not False:
            pl.when(more)(lambda: line_copy(source, chunk, direction).start())
        if chunk >= 2:
            pair_copy(source, chunk, core).start()
        elif chunk == 1:
            precondition(source, 0, lambda p: raw[
                source, p // per_chunk, :, p % per_chunk * LANES:(p % per_chunk + 1) * LANES])
            for done in range(2):
                pair_copy(source, done, core).start()

    def multiply(source, chunk):
        column = chunk - 2
        for arrived in (column, chunk):
            pair_copy(source, arrived, 1 - core).wait_recv()
        block = jnp.concatenate([held[source, column], held[source, chunk]], axis=0)
        part = dot(block, train[:, column * columns:(column + 1) * columns], NT)
        if column == 0:
            acc[source] = part
        else:
            part = part + acc[source]
            part = jnp.concatenate([
                part[(half * CORES + who) * part_rows:(half * CORES + who + 1) * part_rows]
                for who in range(CORES) for half in range(2)], axis=0)

            @pl.when(source // groups == lay)
            def _():
                own[source % groups] = part

            @pl.when(source // groups != lay)
            def _():
                stage[source] = part.astype(BF16)
                lay_copy(source).start()

    def from_right(distance, chunk):
        there = z + distance < z_size
        if chunk >= late:
            there = there & jnp.logical_not(get_late_right & (distance == 1))
        return there

    def from_left(distance, chunk):
        there = (distance >= 1) & (z - distance >= 0)
        if chunk >= late:
            there = there & jnp.logical_not(get_late_left & (distance == 1))
        return there

    def multiply_both(distance, chunk):
        pl.when((distance >= 0) & from_right(distance, chunk))(lambda: multiply(z + distance, chunk))
        pl.when(from_left(distance, chunk))(lambda: multiply(z - distance, chunk))

    loads[-1].wait()

    def step(distance, carry):
        for chunk in range(CHUNKS):
            pl.when((distance >= 1) & from_right(distance, chunk))(
                lambda: forward(z + distance, chunk, -1, has_left))
            pl.when(from_left(distance, chunk))(lambda: forward(z - distance, chunk, 1, has_right))
            if chunk == CHUNKS - 1:
                pl.when(send_late_left & (z + distance == z_size - 1))(lambda: send_late(-1))
                pl.when(send_late_right & (z - distance == 0))(lambda: send_late(1))
            if chunk == 0:
                multiply_both(distance - 1, 3)
            elif chunk == 3:
                multiply_both(distance, 2)
        return carry

    lax.fori_loop(0, z_size, step, 0)
    multiply_both(z_size - 1, CHUNKS - 1)

    def finish(source, direction):
        for chunk in range(late, CHUNKS):
            forward(source, chunk, direction, False)
        for chunk in range(late, CHUNKS):
            multiply(source, chunk)

    pl.when(get_late_right)(lambda: finish(z + 1, -1))
    pl.when(get_late_left)(lambda: finish(z - 1, 1))

    for peer in range(lay_size):
        @pl.when(peer != lay)
        def _():
            for group in range(groups):
                pltpu.make_async_remote_copy(
                    stage.at[0], landed.at[peer, group], send_lay.at[0], recv_lay.at[peer, group],
                    device_id={"lay": peer}, device_id_type=pl.DeviceIdType.MESH).wait_recv()
                own[group] = own[group] + landed[peer, group].astype(F32)
    total = jnp.concatenate([own[group] for group in range(groups)], axis=0)
    score_ref[...] = total.T

    def drain(source, carry):
        @pl.when(source // groups != lay)
        def _():
            lay_copy(source).wait_send()

        for chunk in range(CHUNKS):
            pair_copy(source, chunk, core).wait_send()
            pl.when(has_left & (source >= z))(lambda: line_copy(source, chunk, -1).wait_send())
            pl.when(has_right & (source <= z))(lambda: line_copy(source, chunk, 1).wait_send())
        return carry

    lax.fori_loop(0, z_size, drain, 0)


def solution(mesh):
    z_size, lay_size = mesh.shape["ex"] // CORES, mesh.shape["lay"]

    def on_device(train_grads, query_grads, out_basis, in_basis, eigenvalues):
        examples, width = train_grads.shape[1:]
        count = query_grads.shape[1]
        both = CORES * count
        groups = z_size // lay_size
        side = out_basis.shape[1]
        dma = pltpu.SemaphoreType.DMA
        return pl.pallas_call(
            functools.partial(kernel, z_size, lay_size),
            out_shape=pltpu.VMEM((examples, groups * both), F32),
            in_specs=[pl.BlockSpec(memory_space=pl.ANY)] * 5,
            out_specs=pl.BlockSpec(memory_space=pltpu.VMEM),
            scratch_shapes=[
                pltpu.VMEM((examples, width), BF16),
                pltpu.VMEM(query_grads.shape, BF16),
                pltpu.VMEM(out_basis.shape, F32),
                pltpu.VMEM(in_basis.shape, F32),
                pltpu.VMEM(eigenvalues.shape, F32),
                pltpu.VMEM((z_size, 2, count // 2, width // 2), BF16),
                pltpu.VMEM((z_size, CHUNKS, count, width // 2), BF16),
                pltpu.VMEM((2, 2 * LANES, 2 * LANES), BF16),
                pltpu.VMEM((side, 3 * side), BF16),
                pltpu.VMEM((side, 3 * side), BF16),
                pltpu.VMEM((side, count // 2 * side), F32),
                pltpu.VMEM((count * width // 2 // LANES, LANES), F32),
                pltpu.VMEM((count * width // 2 // LANES, LANES), F32),
                pltpu.VMEM((z_size, both, examples), F32),
                pltpu.VMEM((groups, both, examples), F32),
                pltpu.VMEM((z_size, both, examples), BF16),
                pltpu.VMEM((lay_size, groups, both, examples), BF16),
                dma((5,)),
                dma((z_size, CHUNKS)),
                dma((z_size, CHUNKS)),
                dma((z_size, CHUNKS, 2)),
                dma((z_size, CHUNKS)),
                dma((z_size,)),
                dma((lay_size, groups)),
            ],
            compiler_params=pltpu.CompilerParams(
                collective_id=0, has_side_effects=True, vmem_limit_bytes=58 * 1024 * 1024
            ),
        )(train_grads, query_grads, out_basis, in_basis, eigenvalues)

    in_specs = (
        P("lay", ("grp", "ex"), None),
        P("lay", ("grp", "ex"), None),
        P("lay", None, None),
        P("lay", None, None),
        P("lay", None, None),
    )
    out_specs = P(("grp", "ex"), "lay")
    return jax.shard_map(
        on_device, mesh=mesh, in_specs=in_specs, out_specs=out_specs, check_vma=False
    )
```

```python
import functools

import jax
import jax.numpy as jnp
from jax import lax
from jax.experimental import pallas as pl
from jax.experimental.pallas import tpu as pltpu
from jax.sharding import PartitionSpec as P

DAMPING = 0.1
CORES = 2
CHUNKS = 4
LANES = 128
F32, BF16 = jnp.float32, jnp.bfloat16
NN = (((1,), (0,)), ((), ()))
NT = (((1,), (1,)), ((), ()))


def dot(a, b, dims=NN):
    return lax.dot_general(a, b, dims, preferred_element_type=F32)


def split(x):
    high = x.astype(BF16)
    return high, (x - high.astype(F32)).astype(BF16)


def kernel(z_size, lay_size, train_hbm, query_hbm, out_hbm, in_hbm, eig_hbm, score_ref,
           train, query_ref, out_ref, in_ref, eig_ref, raw, held, mix_ref, to_ref, from_ref, scale_ref,
           by_tile, by_query, acc, own, stage, landed,
           load_sem, recv_line, recv_pair, send_line, send_pair, send_lay, recv_lay):
    ex, lay = lax.axis_index("ex"), lax.axis_index("lay")
    z, core = ex // CORES, ex % CORES
    count, width = query_ref.shape[1:]
    side = out_ref.shape[1]
    tiles = width // LANES
    part_rows = count // 2
    columns = width // 2
    per_chunk = tiles // 2
    groups = z_size // lay_size
    has_left, has_right = z > 0, z < z_size - 1

    late = CHUNKS - 1
    first_slot, last_slot = lay == 1 // groups, lay == (z_size - 2) // groups
    send_late_left, send_late_right = (z == 1) & first_slot, (z == z_size - 2) & last_slot
    get_late_left, get_late_right = (z == z_size - 1) & last_slot, (z == 0) & first_slot

    loads = [pltpu.make_async_copy(*pair, load_sem.at[i]) for i, pair in enumerate((
        (query_hbm, query_ref), (in_hbm, in_ref), (out_hbm, out_ref), (eig_hbm, eig_ref), (train_hbm.at[0], train)))]
    for load in loads:
        load.start()

    barrier = pltpu.get_barrier_semaphore()

    def greet(target):
        pl.semaphore_signal(barrier, inc=1, device_id=target, device_id_type=pl.DeviceIdType.MESH)

    pl.when(has_left)(lambda: greet({"ex": ex - CORES}))
    pl.when(has_right)(lambda: greet({"ex": ex + CORES}))
    greet({"ex": z * CORES + 1 - core})
    for step in range(1, lay_size):
        greet({"lay": (lay + step) % lay_size})

    mine = pl.ds(pl.multiple_of(core * part_rows, part_rows), part_rows)

    def line_copy(source, chunk, direction, own_raw=False):
        block = raw.at[source, chunk] if chunk < 2 else held.at[source, chunk, mine]
        start = query_ref.at[0, pl.ds(0, part_rows), pl.ds(chunk * columns, columns)] if own_raw else block
        return pltpu.make_async_remote_copy(
            start, block, send_line.at[source, chunk, (direction + 1) // 2], recv_line.at[source, chunk],
            device_id={"ex": ex + direction * CORES}, device_id_type=pl.DeviceIdType.MESH)

    def pair_copy(source, chunk, who):
        block = held.at[source, chunk, pl.ds(pl.multiple_of(who * part_rows, part_rows), part_rows)]
        return pltpu.make_async_remote_copy(
            block, block, send_pair.at[source, chunk], recv_pair.at[source, chunk],
            device_id={"ex": z * CORES + 1 - core}, device_id_type=pl.DeviceIdType.MESH)

    def lay_copy(source):
        return pltpu.make_async_remote_copy(
            stage.at[source], landed.at[lay, source % groups], send_lay.at[source],
            recv_lay.at[lay, source % groups],
            device_id={"lay": source // groups}, device_id_type=pl.DeviceIdType.MESH)

    neighbours = has_left.astype(jnp.int32) + has_right.astype(jnp.int32) + lay_size
    pl.semaphore_wait(barrier, neighbours)
    loads[0].wait()
    for chunk in range(2):
        pl.when(has_left)(lambda: line_copy(z, chunk, -1, True).start())
        pl.when(has_right)(lambda: line_copy(z, chunk, 1, True).start())

    for load in loads[1:-1]:
        load.wait()

    half = jnp.concatenate([in_ref[0], in_ref[0]], axis=1)
    low_lane = lax.broadcasted_iota(jnp.int32, half.shape, 1) < side
    zero = jnp.zeros_like(half)
    first, second = jnp.where(low_lane, half, 0.0), jnp.where(low_lane, 0.0, half)
    mix = jnp.concatenate([
        jnp.concatenate([first, zero], axis=1), jnp.concatenate([zero, first], axis=1),
        jnp.concatenate([second, zero], axis=1), jnp.concatenate([zero, second], axis=1)], axis=0)
    mix_high, mix_low = split(mix)
    rows = lax.broadcasted_iota(jnp.int32, (side, side), 0)
    cols = lax.broadcasted_iota(jnp.int32, (side, side), 1)
    order = (cols == 2 * (rows % tiles) + rows // tiles).astype(BF16)
    basis_high, basis_low = split(out_ref[0])
    sorted_high, sorted_low = dot(order, basis_high), dot(order, basis_low)
    to_eigen = jnp.concatenate([sorted_high.T, sorted_high.T, sorted_low.T], axis=1).astype(BF16)
    from_eigen = jnp.concatenate([sorted_high, sorted_high, sorted_low], axis=1).astype(BF16)
    scale = 1.0 / (eig_ref[0] + DAMPING)
    mix_ref[0], mix_ref[1] = mix_high, mix_low
    to_ref[...], from_ref[...] = to_eigen, from_eigen
    scale_ref[...] = jnp.concatenate([scale] * part_rows, axis=1)

    def stacked(x):
        high, low = split(x)
        return jnp.concatenate([high, low, high], axis=0)

    def precondition(source, first_chunk, tile_of):
        for p in range(tiles):
            by_tile[p * part_rows:(p + 1) * part_rows, :] = tile_of(p).astype(F32)
        pairs = jnp.concatenate([
            jnp.concatenate([by_tile[pl.ds(2 * j + i, tiles, stride=part_rows), :] for i in range(2)], axis=1)
            for j in range(part_rows // 2)], axis=0).astype(BF16)
        inner = dot(pairs, mix_ref[0]) + dot(pairs, mix_ref[1])
        inner = jnp.concatenate([
            jnp.concatenate([inner[j * tiles:(j + 1) * tiles, s * LANES:(s + 1) * LANES] for s in range(2)], axis=0)
            for j in range(part_rows // 2)], axis=1)
        rotated = dot(to_ref[...], stacked(inner)) * scale_ref[...]
        back = dot(from_ref[...], stacked(rotated))
        back = jnp.concatenate([
            jnp.concatenate([back[s * tiles:(s + 1) * tiles, j * LANES:(j + 1) * LANES] for s in range(2)], axis=1)
            for j in range(part_rows // 2)], axis=0)
        high, low = split(back)
        result = dot(high, mix_ref[0], NT) + dot(high, mix_ref[1], NT) + dot(low, mix_ref[0], NT)
        for j in range(part_rows // 2):
            for i in range(2):
                at = (2 * j + i) * tiles
                by_query[at:at + tiles, :] = result[j * tiles:(j + 1) * tiles, i * LANES:(i + 1) * LANES]
        for chunk in range(2):
            for t in range(per_chunk):
                tile = by_query[pl.ds(chunk * per_chunk + t, part_rows, stride=tiles), :]
                held[source, first_chunk + chunk, mine, t * LANES:(t + 1) * LANES] = tile.astype(BF16)

    precondition(z, 2, lambda p: query_ref[0, part_rows:, p * LANES:(p + 1) * LANES])
    for chunk in range(2, CHUNKS):
        to_left, to_right = has_left, has_right
        if chunk >= late:
            to_left, to_right = to_left & jnp.logical_not(send_late_left), to_right & jnp.logical_not(send_late_right)
        pl.when(to_left)(lambda: line_copy(z, chunk, -1).start())
        pl.when(to_right)(lambda: line_copy(z, chunk, 1).start())
        pair_copy(z, chunk, core).start()
    precondition(z, 0, lambda p: query_ref[0, :part_rows, p * LANES:(p + 1) * LANES])
    for chunk in range(2):
        pair_copy(z, chunk, core).start()

    def send_late(direction):
        for chunk in range(late, CHUNKS):
            line_copy(z, chunk, direction).start()

    def forward(source, chunk, direction, more):
        line_copy(source, chunk, direction).wait_recv()
        if more is not False:
            pl.when(more)(lambda: line_copy(source, chunk, direction).start())
        if chunk >= 2:
            pair_copy(source, chunk, core).start()
        elif chunk == 1:
            precondition(source, 0, lambda p: raw[
                source, p // per_chunk, :, p % per_chunk * LANES:(p % per_chunk + 1) * LANES])
            for done in range(2):
                pair_copy(source, done, core).start()

    def multiply(source, chunk):
        column = chunk - 2
        for arrived in (column, chunk):
            pair_copy(source, arrived, 1 - core).wait_recv()
        block = jnp.concatenate([held[source, column], held[source, chunk]], axis=0)
        part = dot(block, train[:, column * columns:(column + 1) * columns], NT)
        if column == 0:
            acc[source] = part
        else:
            part = part + acc[source]
            part = jnp.concatenate([
                part[(half * CORES + who) * part_rows:(half * CORES + who + 1) * part_rows]
                for who in range(CORES) for half in range(2)], axis=0)

            @pl.when(source // groups == lay)
            def _():
                own[source % groups] = part

            @pl.when(source // groups != lay)
            def _():
                stage[source] = part.astype(BF16)
                lay_copy(source).start()

    def from_right(distance, chunk):
        there = z + distance < z_size
        if chunk >= late:
            there = there & jnp.logical_not(get_late_right & (distance == 1))
        return there

    def from_left(distance, chunk):
        there = (distance >= 1) & (z - distance >= 0)
        if chunk >= late:
            there = there & jnp.logical_not(get_late_left & (distance == 1))
        return there

    def multiply_both(distance, chunk):
        pl.when((distance >= 0) & from_right(distance, chunk))(lambda: multiply(z + distance, chunk))
        pl.when(from_left(distance, chunk))(lambda: multiply(z - distance, chunk))

    loads[-1].wait()

    def step(distance, carry):
        for chunk in range(CHUNKS):
            pl.when((distance >= 1) & from_right(distance, chunk))(
                lambda: forward(z + distance, chunk, -1, has_left))
            pl.when(from_left(distance, chunk))(lambda: forward(z - distance, chunk, 1, has_right))
            if chunk == CHUNKS - 1:
                pl.when(send_late_left & (z + distance == z_size - 1))(lambda: send_late(-1))
                pl.when(send_late_right & (z - distance == 0))(lambda: send_late(1))
            if chunk == 0:
                multiply_both(distance - 1, 3)
            elif chunk == 3:
                multiply_both(distance, 2)
        return carry

    lax.fori_loop(0, z_size, step, 0)
    multiply_both(z_size - 1, CHUNKS - 1)

    def finish(source, direction):
        for chunk in range(late, CHUNKS):
            forward(source, chunk, direction, False)
        for chunk in range(late, CHUNKS):
            multiply(source, chunk)

    pl.when(get_late_right)(lambda: finish(z + 1, -1))
    pl.when(get_late_left)(lambda: finish(z - 1, 1))

    for peer in range(lay_size):
        @pl.when(peer != lay)
        def _():
            for group in range(groups):
                pltpu.make_async_remote_copy(
                    stage.at[0], landed.at[peer, group], send_lay.at[0], recv_lay.at[peer, group],
                    device_id={"lay": peer}, device_id_type=pl.DeviceIdType.MESH).wait_recv()
                own[group] = own[group] + landed[peer, group].astype(F32)
    total = jnp.concatenate([own[group] for group in range(groups)], axis=0)
    score_ref[...] = total.T

    def drain(source, carry):
        @pl.when(source // groups != lay)
        def _():
            lay_copy(source).wait_send()

        for chunk in range(CHUNKS):
            pair_copy(source, chunk, core).wait_send()
            pl.when(has_left & (source >= z))(lambda: line_copy(source, chunk, -1).wait_send())
            pl.when(has_right & (source <= z))(lambda: line_copy(source, chunk, 1).wait_send())
        return carry

    lax.fori_loop(0, z_size, drain, 0)


def solution(mesh):
    z_size, lay_size = mesh.shape["ex"] // CORES, mesh.shape["lay"]

    def on_device(train_grads, query_grads, out_basis, in_basis, eigenvalues):
        examples, width = train_grads.shape[1:]
        count = query_grads.shape[1]
        both = CORES * count
        groups = z_size // lay_size
        side = out_basis.shape[1]
        dma = pltpu.SemaphoreType.DMA
        return pl.pallas_call(
            functools.partial(kernel, z_size, lay_size),
            out_shape=pltpu.VMEM((examples, groups * both), F32),
            in_specs=[pl.BlockSpec(memory_space=pl.ANY)] * 5,
            out_specs=pl.BlockSpec(memory_space=pltpu.VMEM),
            scratch_shapes=[
                pltpu.VMEM((examples, width), BF16),
                pltpu.VMEM(query_grads.shape, BF16),
                pltpu.VMEM(out_basis.shape, F32),
                pltpu.VMEM(in_basis.shape, F32),
                pltpu.VMEM(eigenvalues.shape, F32),
                pltpu.VMEM((z_size, 2, count // 2, width // 2), BF16),
                pltpu.VMEM((z_size, CHUNKS, count, width // 2), BF16),
                pltpu.VMEM((2, 2 * LANES, 2 * LANES), BF16),
                pltpu.VMEM((side, 3 * side), BF16),
                pltpu.VMEM((side, 3 * side), BF16),
                pltpu.VMEM((side, count // 2 * side), F32),
                pltpu.VMEM((count * width // 2 // LANES, LANES), F32),
                pltpu.VMEM((count * width // 2 // LANES, LANES), F32),
                pltpu.VMEM((z_size, both, examples), F32),
                pltpu.VMEM((groups, both, examples), F32),
                pltpu.VMEM((z_size, both, examples), BF16),
                pltpu.VMEM((lay_size, groups, both, examples), BF16),
                dma((5,)),
                dma((z_size, CHUNKS)),
                dma((z_size, CHUNKS)),
                dma((z_size, CHUNKS, 2)),
                dma((z_size, CHUNKS)),
                dma((z_size,)),
                dma((lay_size, groups)),
            ],
            compiler_params=pltpu.CompilerParams(
                collective_id=0, has_side_effects=True, vmem_limit_bytes=58 * 1024 * 1024
            ),
        )(train_grads, query_grads, out_basis, in_basis, eigenvalues)

    in_specs = (
        P("lay", ("grp", "ex"), None),
        P("lay", ("grp", "ex"), None),
        P("lay", None, None),
        P("lay", None, None),
        P("lay", None, None),
    )
    out_specs = P(("grp", "ex"), "lay")
    return jax.shard_map(
        on_device, mesh=mesh, in_specs=in_specs, out_specs=out_specs, check_vma=False
    )
```
